256 devices in a mesh: replica: 8 (over z_lo, x), tensor: 32 (over z_hi, y, core).
Axes of the slice: x: 4, y: 4, z: 8 (z_hi: 4, z_lo: 2; z = z_hi * 2 + z_lo), core: 2. Of those that a mesh axis runs over, the one named last changes fastest.
Arguments:
- tokens: bfloat16 [4096, 4096], P('replica', 'tensor'), may hold values from -6 to 6
- prev_gain: float32 [4096], replicated, may hold values from 0.1 to 1.9
- prev_gate_up: bfloat16 [4096, 2, 16384], P(None, None, 'tensor'), may hold values from -0.09375 to 0.09375
- prev_down: bfloat16 [16384, 4096], P('tensor', 'replica'), may hold values from -0.046875 to 0.046875
- next_gain: float32 [4096], replicated, may hold values from 0.1 to 1.9
- piece_buffer: bfloat16 [6144, 2, 16384], P('replica', None, 'tensor'), may hold values from -0.09375 to 0.09375
- slot_rows: int32 [6144], replicated, may hold values from 0 to 4096, as said below
- next_down: bfloat16 [16384, 4096], P('tensor', 'replica'), may hold values from -0.046875 to 0.046875
- score_head: float32 [4096, 2], P('tensor'), may hold values from -0.09375 to 0.09375
- step_positions: int32 [192], P('replica'), may hold values from 0 to 511, as said below
Outputs:
- layer_out: bfloat16 [4096, 4096], P('replica', 'tensor')
- step_logits: float32 [192, 2], P('replica')
The draws below stay inside these ranges and needn't reach their ends.
Inputs may be any that keep to these rules, and one draw needn't show every extreme that they name: `slot_rows`: every row 0 to 4095 stands in exactly one slot. Slots r * 768 to (r + 1) * 768 - 1 belong to replica r; its filled slots come first, the rest hold 4096; some replica has all 768 slots filled. `step_positions`: within each replica's 24 entries the positions are distinct and rising; the first is 0 and the last is 511.
All inputs are finite; a program needn't handle non-finite values.
Results may differ from the reference program's by a relative error of at most 0.025.
Values may be sent and summed in bfloat16 or wider, within the bound.
A program may use at most 128 MiB of HBM per device.

```python
import jax
import jax.numpy as jnp
from jax import lax

D = 4096
FFW = 16384
ROWS_REP = 512
STEPS_REP = 24
TOKENS = 4096
STEPS = 192
BASE = 512
CAP = 768
SLOTS = 6144
N_REPLICA = 8
N_TENSOR = 32


def draw_slot_rows(key, part):
    key = jax.random.fold_in(key, 11)
    first_key, second_key, third_key = jax.random.split(key, 3)
    row_order = jax.random.permutation(first_key, D).astype(jnp.int32)
    pairing = jax.random.permutation(second_key, N_REPLICA).astype(jnp.int32)
    shifts_pair = jax.random.randint(third_key, (N_REPLICA // 2,), 0, BASE // 2 + 1).astype(jnp.int32)
    shifts_pair = shifts_pair.at[0].set(BASE // 2)
    counts = jnp.zeros((N_REPLICA,), jnp.int32)
    counts = counts.at[pairing[0::2]].set(BASE + shifts_pair)
    counts = counts.at[pairing[1::2]].set(BASE - shifts_pair)
    offsets = jnp.cumsum(counts) - counts
    slot_range = jnp.arange(CAP, dtype=jnp.int32)
    within = slot_range[None, :] < counts[:, None]
    source_index = jnp.minimum(offsets[:, None] + slot_range[None, :], D - 1)
    filled_rows = jnp.where(within, row_order[source_index], D)
    return filled_rows.reshape(-1).astype(jnp.int32)


def draw_step_positions(key, part):
    key = jax.random.fold_in(key, 23)
    replica_keys = jax.random.split(key, N_REPLICA)

    def pick_positions(sub_key):
        chosen = jax.random.permutation(sub_key, ROWS_REP - 2)[:STEPS_REP - 2] + 1
        chosen = jnp.sort(chosen.astype(jnp.int32))
        return jnp.concatenate([jnp.zeros((1,), jnp.int32), chosen, jnp.full((1,), ROWS_REP - 1, jnp.int32)])
    return jax.vmap(pick_positions)(replica_keys).reshape(-1).astype(jnp.int32)


def level_of(own_key, dims, pieces, low, top_value):
    factor_of = 1.0
    for position, parts in pieces:
        draws = jax.random.uniform(jax.random.fold_in(jax.random.fold_in(own_key, 6), position), (parts,), jnp.float32, low / len(pieces), top_value / len(pieces))
        factor_of = factor_of * jnp.repeat(jnp.exp(draws), dims[position] // parts).reshape((-1,) + (1,) * (len(dims) - 1 - position))
    return factor_of


def noise(key, dims, spread, bound, cuts=(), kind=jnp.bfloat16):
    array = spread * jax.random.normal(key, dims, jnp.float32)
    if cuts:
        array = array * level_of(key, dims, cuts, -0.22, 0.18)
    return jnp.clip(array, -bound, bound).astype(kind)


def setup_inputs(seed: int = 0) -> dict:
    key_of = jax.random.split(jax.random.key(seed), 11)
    return {
        "tokens": noise(key_of[0], (TOKENS, D), 1.0, 6.0, ((0, 8), (1, 32))),
        "prev_gain": jnp.clip(1.0 + 0.18 * jax.random.normal(key_of[1], (D,), jnp.float32), 0.1, 1.9),
        "prev_gate_up": noise(key_of[2], (D, 2, FFW), D ** -0.5, 0.09375, ((2, 32),)),
        "prev_down": noise(key_of[3], (FFW, D), FFW ** -0.5, 0.046875, ((0, 32), (1, 8))),
        "next_gain": jnp.clip(1.0 + 0.18 * jax.random.normal(key_of[4], (D,), jnp.float32), 0.1, 1.9),
        "piece_buffer": noise(key_of[5], (SLOTS, 2, FFW), D ** -0.5, 0.09375, ((0, 8), (2, 32))),
        "slot_rows": draw_slot_rows(jax.random.fold_in(key_of[10], 71), 0),
        "next_down": noise(key_of[7], (FFW, D), FFW ** -0.5, 0.046875, ((0, 32), (1, 8))),
        "score_head": noise(key_of[8], (D, 2), D ** -0.5, 0.09375, ((0, 32),), jnp.float32),
        "step_positions": draw_step_positions(jax.random.fold_in(key_of[10], 71), 0),
    }


def normalize(values, gain):
    floats = values.astype(jnp.float32)
    scale = lax.rsqrt(lax.optimization_barrier(jnp.mean(floats * floats, axis=-1, keepdims=True)) + 1e-06)
    return (floats * scale * gain).astype(jnp.bfloat16)

def swiglu(normed, gate_up):
    both = jnp.dot(normed, gate_up.reshape(D, 2 * FFW), preferred_element_type=jnp.float32)
    both = both.reshape(-1, 2, FFW)
    return (jax.nn.silu(both[:, 0]) * both[:, 1]).astype(jnp.bfloat16)

def down_sum(hidden, down):
    block = FFW // N_TENSOR

    def add_block(carry, index):
        hid_block = lax.dynamic_slice_in_dim(hidden, index * block, block, 1)
        down_block = lax.dynamic_slice_in_dim(down, index * block, block, 0)
        rounded = jnp.dot(hid_block, down_block, preferred_element_type=jnp.float32).astype(jnp.bfloat16)
        rounded = lax.optimization_barrier(rounded)
        return (carry + rounded.astype(jnp.float32), None)
    start = jnp.zeros((hidden.shape[0], D), jnp.float32)
    summed, _ = lax.scan(add_block, start, jnp.arange(N_TENSOR, dtype=jnp.int32))
    return summed

def reference(tokens, prev_gain, prev_gate_up, prev_down, next_gain, piece_buffer, slot_rows, next_down, score_head, step_positions):
    hidden = swiglu(normalize(tokens, prev_gain), prev_gate_up)
    middle = (tokens.astype(jnp.float32) + down_sum(hidden, prev_down)).astype(jnp.bfloat16)
    assembled = jnp.zeros((D + 1, 2, FFW), piece_buffer.dtype).at[slot_rows].set(piece_buffer)[:D]
    hidden_next = swiglu(normalize(middle, next_gain), assembled)
    layer_out = (middle.astype(jnp.float32) + down_sum(hidden_next, next_down)).astype(jnp.bfloat16)
    owner = jnp.arange(STEPS, dtype=jnp.int32) // STEPS_REP
    picked = layer_out[step_positions + owner * ROWS_REP].astype(jnp.float32)
    step_logits = jnp.dot(picked, score_head, precision=lax.Precision.HIGHEST)
    return (layer_out, step_logits)
```

```python
import jax
import jax.numpy as jnp
from jax import lax
from jax.experimental import pallas as pl
from jax.experimental.pallas import tpu as pltpu
from jax.sharding import PartitionSpec as P

MESH = pl.DeviceIdType.MESH
BF = jnp.bfloat16
F32 = jnp.float32
D = 4096
T = 512
H = T // 2
W = 512
CAP = 768
SLOTS = 8 * CAP
N_SEM = 160
RAW = 256
RAW_SLOTS = 4


def kernel(
    tok_in, gain1, gate_up, down1_in, gain2, piece_in, slots, down2_in, head, pos,
    out, logits,
    act, wprev, raw, down1, down2, pcs, nperm, nbuf, both, hid, sumsq,
    prt, rs_c, y_l, y_r, yt_l, yt_r, z_l, z_r, zt_l, zt_r, lgs,
    ssem, rsem, lsem, raw_sem,
):
    rep = lax.axis_index("replica")
    ten = lax.axis_index("tensor")
    ml, mx = rep // 4, rep % 4
    mz, my, mc = ten // 8, (ten // 2) % 4, ten % 2

    def at(zl=ml, x=mx, z=mz, y=my, c=mc):
        return (zl * 4 + x, (z * 4 + y) * 2 + c)

    def mod4(v):
        return lax.rem(v + 4, 4)

    x_right, x_left = at(x=mod4(mx + 1)), at(x=mod4(mx - 1))
    y_right, y_left = at(y=mod4(my + 1)), at(y=mod4(my - 1))
    z_right, z_left = at(z=mod4(mz + 1)), at(z=mod4(mz - 1))
    sibling = at(c=1 - mc)
    partner = at(zl=1 - ml)

    count = [0]
    unsent = []
    unsent_weights = []

    def send(src, dst, device, pending=unsent):
        i = count[0]
        count[0] += 1
        copy = pltpu.make_async_remote_copy(
            src_ref=src, dst_ref=dst, send_sem=ssem.at[i], recv_sem=rsem.at[i],
            device_id=device, device_id_type=MESH,
        )
        copy.start()
        pending.append(copy)
        return copy

    def drain(pending=unsent):
        for copy in pending:
            copy.wait_send()
        pending.clear()

    def send_weights(src, dst, device):
        return send(src, dst, device, unsent_weights)

    own = act.at[mz, mc, my]
    loads = [
        pltpu.make_async_copy(tok_in, own, lsem.at[0]),
        pltpu.make_async_copy(down1_in, down1.at[rep], lsem.at[1]),
        pltpu.make_async_copy(down2_in, down2.at[rep], lsem.at[2]),
    ]
    for load in loads:
        load.start()

    order = [mz, mod4(mz - 1), mod4(mz + 1), mod4(mz + 2)]
    n_piece = CAP // RAW
    n_raw = n_piece + D // RAW

    def raw_copy(i):
        if i < n_piece:
            src = piece_in.at[pl.ds(i * RAW, RAW)]
        else:
            j = i - n_piece
            src = gate_up.at[pl.ds(pl.multiple_of(order[j // 4] * 1024 + (j % 4) * RAW, RAW), RAW)]
        return pltpu.make_async_copy(src, raw.at[i % RAW_SLOTS], raw_sem.at[i % RAW_SLOTS])

    for i in range(RAW_SLOTS):
        raw_copy(i).start()

    barrier = pltpu.get_barrier_semaphore()
    neighbours = (x_right, x_left, y_right, y_left, z_right, z_left, sibling, partner)
    for n in neighbours:
        pl.semaphore_signal(barrier, inc=1, device_id=n, device_id_type=MESH)

    done = [0]

    def relay(n):
        for _ in range(n):
            i = done[0]
            if i >= n_raw:
                return
            done[0] += 1
            raw_copy(i).wait()
            slot = i % RAW_SLOTS

            def step(k, _):
                rows = pl.ds(pl.multiple_of(k * 64, 64), 64)
                flat = raw[slot, rows].reshape(64, 2 * W)
                if i < n_piece:
                    pcs[rep, pl.ds(pl.multiple_of(i * RAW + k * 64, 64), 64), :] = flat
                else:
                    j = i - n_piece
                    base = order[j // 4] * 1024 + (j % 4) * RAW + k * 64
                    wprev[pl.ds(pl.multiple_of(base, 64), 64), :] = flat
                return 0

            lax.fori_loop(0, RAW // 64, step, 0)
            if i + RAW_SLOTS < n_raw:
                raw_copy(i + RAW_SLOTS).start()

    def gather(buf, half):
        def halves(b):
            return buf.at[b, pl.ds(0, half)], buf.at[b, pl.ds(half, half)]

        left, right, far = mod4(mx - 1), mod4(mx + 1), mod4(mx + 2)
        me = ml * 4
        other = (1 - ml) * 4
        h = {}

        def start():
            b = buf.at[me + mx]
            h["p"] = send_weights(b, b, partner)
            h["r"] = send_weights(b, b, x_right)
            h["l"] = send_weights(b, b, x_left)

        def forward():
            h["r"].wait_recv()
            a, _ = halves(me + left)
            h["ra"] = send_weights(a, a, x_right)
            h["l"].wait_recv()
            _, b = halves(me + right)
            h["lb"] = send_weights(b, b, x_left)

        def relay_partner():
            h["p"].wait_recv()
            b = buf.at[other + mx]
            h["pr"] = send_weights(b, b, x_right)
            h["pl"] = send_weights(b, b, x_left)

        def forward_partner():
            h["pr"].wait_recv()
            a, _ = halves(other + left)
            h["pra"] = send_weights(a, a, x_right)
            h["pl"].wait_recv()
            _, b = halves(other + right)
            h["plb"] = send_weights(b, b, x_left)

        def far_to_partner():
            h["ra"].wait_recv()
            h["lb"].wait_recv()
            b = buf.at[me + far]
            h["pf"] = send_weights(b, b, partner)

        def wait(*names):
            for n in names:
                h[n].wait_recv()

        index = {
            "own": me + mx, "left": me + left, "right": me + right, "far": me + far,
            "pown": other + mx, "pleft": other + left, "pright": other + right, "pfar": other + far,
        }
        return start, forward, relay_partner, forward_partner, far_to_partner, wait, index

    g1 = gather(down1, 256)
    gp = gather(pcs, CAP // 2)
    g2 = gather(down2, 256)

    def blk(q, y=my):
        return act.at[q, mc, y]

    def half_a(ref):
        return ref.at[pl.ds(0, H)]

    def half_b(ref):
        return ref.at[pl.ds(H, H)]

    def activations():
        h = {}
        qz = dict(zip(("own", "left", "right", "far"), order))

        def y_start(k):
            b = blk(qz[k])
            h[k, "r"] = send(b, b, y_right)
            h[k, "l"] = send(b, b, y_left)

        def y_forward(k):
            h[k, "r"].wait_recv()
            a = half_a(blk(qz[k], mod4(my - 1)))
            h[k, "ra"] = send(a, a, y_right)
            h[k, "l"].wait_recv()
            b = half_b(blk(qz[k], mod4(my + 1)))
            h[k, "lb"] = send(b, b, y_left)

        def y_end(k):
            h[k, "ra"].wait_recv()
            h[k, "lb"].wait_recv()
            b = act.at[qz[k], mc]
            h[k, "c"] = send(b, b, sibling)

        def z_start():
            b = blk(mz)
            h["r"] = send(b, b, z_right)
            h["l"] = send(b, b, z_left)

        def z_left_in():
            h["r"].wait_recv()
            a = half_a(blk(qz["left"]))
            h["ra"] = send(a, a, z_right)

        def z_right_in():
            h["l"].wait_recv()
            b = half_b(blk(qz["right"]))
            h["lb"] = send(b, b, z_left)

        def z_end():
            h["ra"].wait_recv()
            h["lb"].wait_recv()

        def whole(k):
            h[k, "c"].wait_recv()

        return y_start, y_forward, y_end, z_start, z_left_in, z_right_in, z_end, whole

    def scaled(q, gain):
        def step(i, _):
            v = act[q, lax.rem(i, 2), i // 2].astype(F32)
            g = gain[pl.ds(q * 8 + i, 1), :]
            nbuf[:, pl.ds(pl.multiple_of(i * 128, 128), 128)] = (v * g).astype(BF)
            sumsq[...] += v * v
            return 0

        lax.fori_loop(0, 8, step, 0)

    def mm_prev(q):
        rows = pl.ds(pl.multiple_of(q * 1024, 1024), 1024)

        def step(j, _):
            cols = pl.ds(pl.multiple_of(j * 256, 256), 256)
            both[:, cols] += jnp.dot(nbuf[...], wprev[rows, cols], preferred_element_type=F32)
            return 0

        lax.fori_loop(0, 4, step, 0)

    def permute(q, first):
        def step(s, _):
            want = slots[pl.ds(s, 1), :] - q * 1024
            rows = lax.broadcasted_iota(jnp.int32, (1024, 256), 0)
            pick = jnp.where(rows == want, 1.0, 0.0).astype(BF)
            moved = jnp.dot(nbuf[...], pick, preferred_element_type=F32)
            if first:
                nperm[s] = moved.astype(BF)
            else:
                nperm[s] = (nperm[s].astype(F32) + moved).astype(BF)
            return 0

        lax.fori_loop(0, SLOTS // 256, step, 0)

    def mm_piece(r):
        def step(j, _):
            cols = pl.ds(pl.multiple_of(j * 256, 256), 256)
            total = both[:, cols]
            for k in range(3):
                total += jnp.dot(
                    nperm[r * 3 + k], pcs[r, pl.ds(k * 256, 256), cols], preferred_element_type=F32
                )
            both[:, cols] = total
            return 0

        lax.fori_loop(0, 4, step, 0)

    def hidden():
        def step(i, _):
            rows = pl.ds(pl.multiple_of(i * 64, 64), 64)
            mean = jnp.sum(sumsq[rows, :], axis=1, keepdims=True) * (1.0 / D)
            scale = lax.rsqrt(mean + 1e-06)
            g = both[rows, pl.ds(0, W)] * scale
            u = both[rows, pl.ds(W, W)] * scale
            hid[rows, :] = (g / (1.0 + jnp.exp(-g)) * u).astype(BF)
            return 0

        lax.fori_loop(0, T // 64, step, 0)

    def reset():
        both[...] = jnp.zeros_like(both)
        sumsq[...] = jnp.zeros_like(sumsq)

    def add(dst, *srcs):
        total = dst[...].astype(F32)
        for s in srcs:
            total += s[...].astype(F32)
        dst[...] = total.astype(BF)

    def reduce(down, ready, extra):
        groups = [mod4(mz + 2), mod4(mz + 1), mod4(mz - 1), mz]
        c_in = {}
        t_in = {}
        y_in = {}
        z_in = {}

        def mult(k):
            q = groups[k]
            ready(k)

            def step(y, _):
                cols = pl.ds(pl.multiple_of(lax.rem(y, 2) * 256, 256), 256)
                term = jnp.dot(hid[...], down[q * 2 + y // 2, :, cols], preferred_element_type=F32)
                prt[q, 0, y] = term[:, :128].astype(BF)
                prt[q, 1, y] = term[:, 128:].astype(BF)
                return 0

            lax.fori_loop(0, 4, step, 0)
            c_in[k] = send(prt.at[q, 1 - mc], rs_c.at[k], sibling)

        def cores(k):
            q = groups[k]
            c_in[k].wait_recv()

            def step(y, _):
                add(prt.at[q, mc, y], rs_c.at[k, y])
                return 0

            lax.fori_loop(0, 4, step, 0)
            far = prt.at[q, mc, mod4(my + 2)]
            t_in[k] = (
                send(half_a(far), yt_l.at[k], y_right),
                send(half_b(far), yt_r.at[k], y_left),
            )

        def y_pass(k):
            q = groups[k]
            t_in[k][0].wait_recv()
            right = prt.at[q, mc, mod4(my + 1)]
            add(half_a(right), yt_l.at[k])
            first = send(right, y_l.at[k], y_right)
            t_in[k][1].wait_recv()
            left = prt.at[q, mc, mod4(my - 1)]
            add(half_b(left), yt_r.at[k])
            second = send(left, y_r.at[k], y_left)
            y_in[k] = (first, second)

        def y_last(k):
            q = groups[k]
            y_in[k][0].wait_recv()
            y_in[k][1].wait_recv()
            mine = prt.at[q, mc, my]
            add(mine, y_l.at[k], y_r.at[k])
            if k == 0:
                z_in["a"] = send(half_a(mine), zt_l, z_right)
                z_in["b"] = send(half_b(mine), zt_r, z_left)
            elif k == 1:
                z_in["a"].wait_recv()
                add(half_a(mine), zt_l)
                z_in["l"] = send(mine, z_l, z_right)
            elif k == 2:
                z_in["b"].wait_recv()
                add(half_b(mine), zt_r)
                z_in["r"] = send(mine, z_r, z_left)
            else:
                z_in["l"].wait_recv()
                z_in["r"].wait_recv()

        mult(0)
        mult(1)
        cores(0)
        mult(2)
        cores(1)
        y_pass(0)
        mult(3)
        cores(2)
        y_pass(1)
        y_last(0)
        cores(3)
        extra(0)
        y_pass(2)
        y_last(1)
        y_pass(3)
        extra(1)
        y_last(2)
        y_last(3)
        total = act[mz, mc, my].astype(F32) + prt[mz, mc, my].astype(F32)
        return (total + z_l[...].astype(F32) + z_r[...].astype(F32)).astype(BF)

    reset()
    pl.semaphore_wait(barrier, len(neighbours))
    loads[0].wait()
    y_start, y_forward, y_end, z_start, z_left_in, z_right_in, z_end, whole = activations()
    z_start()
    y_start("own")
    loads[1].wait()
    g1[0]()
    relay(5)
    z_left_in()
    y_start("left")
    z_right_in()
    y_start("right")
    relay(2)
    y_forward("own")
    relay(2)
    y_forward("left")
    z_end()
    y_start("far")
    g1[1]()
    relay(2)
    y_end("own")
    y_forward("right")
    relay(2)
    g1[2]()
    y_end("left")
    y_forward("far")
    relay(6)
    loads[2].wait()
    whole("own")
    scaled(order[0], gain1)
    mm_prev(order[0])
    y_end("right")
    whole("left")
    scaled(order[1], gain1)
    mm_prev(order[1])
    y_end("far")
    g1[3]()
    gp[0]()
    whole("right")
    scaled(order[2], gain1)
    mm_prev(order[2])
    whole("far")
    scaled(order[3], gain1)
    mm_prev(order[3])
    hidden()
    drain()

    def ready1(k):
        if k == 0:
            g1[5]("ra", "lb", "pra", "plb")

    def extra1(k):
        if k == 0:
            gp[1]()
        if k == 1:
            gp[2]()

    middle = reduce(down1, ready1, extra1)
    own[...] = middle

    reset()
    y_start, y_forward, y_end, z_start, z_left_in, z_right_in, z_end, whole = activations()
    z_start()
    y_start("own")
    g2[0]()
    z_left_in()
    y_start("left")
    z_right_in()
    y_start("right")
    y_forward("own")
    y_forward("left")
    z_end()
    y_start("far")
    y_end("own")
    y_forward("right")
    whole("own")
    scaled(order[0], gain2)
    permute(order[0], True)
    y_end("left")
    y_forward("far")
    gp[4]()
    whole("left")
    scaled(order[1], gain2)
    permute(order[1], False)
    y_end("right")
    whole("right")
    scaled(order[2], gain2)
    permute(order[2], False)
    y_end("far")
    g2[1]()
    whole("far")
    scaled(order[3], gain2)
    permute(order[3], False)
    drain()
    index = gp[6]
    mm_piece(index["own"])
    mm_piece(index["left"])
    mm_piece(index["right"])
    mm_piece(index["far"])
    mm_piece(index["pown"])
    g2[2]()
    gp[5]("pr")
    mm_piece(index["pleft"])
    gp[5]("pl")
    mm_piece(index["pright"])
    gp[5]("pf")
    mm_piece(index["pfar"])
    hidden()
    g2[4]()

    def ready2(k):
        if k == 0:
            g2[5]("pr", "pl", "pf")

    last = reduce(down2, ready2, lambda k: None)
    out[...] = last

    lanes = lax.broadcasted_iota(jnp.int32, (24, T), 1)
    pick = jnp.where(lanes == pos[...], 1.0, 0.0).astype(BF)
    picked = jnp.dot(pick, last, preferred_element_type=F32)
    first = jnp.sum(picked * head[pl.ds(0, 1), :], axis=1, keepdims=True)
    second = jnp.sum(picked * head[pl.ds(1, 1), :], axis=1, keepdims=True)
    lane = lax.broadcasted_iota(jnp.int32, (24, 128), 1)
    lgs[0] = jnp.where(lane == 0, first, jnp.where(lane == 1, second, 0.0))
    a = send(lgs.at[0], lgs.at[1], sibling)
    a.wait_recv()
    lgs[2] = lgs[0] + lgs[1]
    base = 2
    for right, left in ((y_right, y_left), (z_right, z_left)):
        a = send(lgs.at[base], lgs.at[base + 1], right)
        b = send(lgs.at[base], lgs.at[base + 2], left)
        a.wait_recv()
        c = send(lgs.at[base + 1], lgs.at[base + 3], right)
        b.wait_recv()
        c.wait_recv()
        lgs[base + 4] = (lgs[base] + lgs[base + 3]) + (lgs[base + 1] + lgs[base + 2])
        base += 4
    logits[...] = lgs[base][:, :2]
    drain()
    drain(unsent_weights)


def shards(
    tokens, prev_gain, prev_gate_up, prev_down, next_gain, piece_buffer, slot_rows, next_down,
    score_head, step_positions,
):
    hbm = pl.BlockSpec(memory_space=pl.ANY)
    vmem = pl.BlockSpec(memory_space=pltpu.VMEM)
    dma = pltpu.SemaphoreType.DMA
    block = (T, 128)
    return pl.pallas_call(
        kernel,
        out_shape=(
            jax.ShapeDtypeStruct((T, 128), BF),
            jax.ShapeDtypeStruct((24, 2), F32),
        ),
        in_specs=[hbm, vmem, hbm, hbm, vmem, hbm, vmem, hbm, vmem, vmem],
        out_specs=(vmem, vmem),
        scratch_shapes=[
            pltpu.VMEM((4, 2, 4) + block, BF),
            pltpu.VMEM((D, 2 * W), BF),
            pltpu.VMEM((RAW_SLOTS, RAW, 2, W), BF),
            pltpu.VMEM((8, W, 512), BF),
            pltpu.VMEM((8, W, 512), BF),
            pltpu.VMEM((8, CAP, 2 * W), BF),
            pltpu.VMEM((SLOTS // 256, T, 256), BF),
            pltpu.VMEM((T, 1024), BF),
            pltpu.VMEM((T, 2 * W), F32),
            pltpu.VMEM((T, W), BF),
            pltpu.VMEM(block, F32),
            pltpu.VMEM((4, 2, 4) + block, BF),
            pltpu.VMEM((4, 4) + block, BF),
            pltpu.VMEM((4,) + block, BF),
            pltpu.VMEM((4,) + block, BF),
            pltpu.VMEM((4, H, 128), BF),
            pltpu.VMEM((4, H, 128), BF),
            pltpu.VMEM(block, BF),
            pltpu.VMEM(block, BF),
            pltpu.VMEM((H, 128), BF),
            pltpu.VMEM((H, 128), BF),
            pltpu.VMEM((11, 24, 128), F32),
            dma((N_SEM,)),
            dma((N_SEM,)),
            dma((3,)),
            dma((RAW_SLOTS,)),
        ],
        compiler_params=pltpu.CompilerParams(
            collective_id=0, has_side_effects=True, vmem_limit_bytes=62 * 2**20
        ),
        cost_estimate=pl.CostEstimate(
            flops=2 * T * (D * 1024 + SLOTS * 1024 + D * SLOTS + 2 * 512 * D),
            bytes_accessed=16 * 2**20, transcendentals=2 * T * W,
        ),
    )(
        tokens,
        prev_gain.reshape(32, 128),
        prev_gate_up,
        prev_down,
        next_gain.reshape(32, 128),
        piece_buffer,
        slot_rows.reshape(SLOTS // 256, 256),
        next_down,
        score_head.T,
        step_positions.reshape(24, 1),
    )


def solution(mesh):
    in_specs = (
        P("replica", "tensor"),
        P(),
        P(None, None, "tensor"),
        P("tensor", "replica"),
        P(),
        P("replica", None, "tensor"),
        P(),
        P("tensor", "replica"),
        P("tensor", None),
        P("replica"),
    )
    out_specs = (P("replica", "tensor"), P("replica", None))
    return jax.shard_map(shards, mesh=mesh, in_specs=in_specs, out_specs=out_specs, check_vma=False)
```

```python
import jax
import jax.numpy as jnp
from jax import lax
from jax.experimental import pallas as pl
from jax.experimental.pallas import tpu as pltpu
from jax.sharding import PartitionSpec as P

MESH = pl.DeviceIdType.MESH
BF = jnp.bfloat16
F32 = jnp.float32
D = 4096
T = 512
H = T // 2
ROWS = T + 16
W = 512
CAP = 768
SLOTS = 8 * CAP
N_SEM = 192
RAW = 256
RAW_SLOTS = 4


def kernel(
    tok_in, gain1, gate_up, down1_in, gain2, piece_in, slots, down2_in, head, pos,
    out, logits,
    act, score, wprev, raw, down1, down2, pcs, nperm, rowid, nbuf, both, hid, sumsq,
    prt, rs_c, y_l, y_r, yt_l, yt_r, z_l, z_r, zt_l, zt_r, lgs,
    ssem, rsem, lsem, raw_sem,
):
    rep = lax.axis_index("replica")
    ten = lax.axis_index("tensor")
    ml, mx = rep // 4, rep % 4
    mz, my, mc = ten // 8, (ten // 2) % 4, ten % 2

    def at(zl=ml, x=mx, z=mz, y=my, c=mc):
        return (zl * 4 + x, (z * 4 + y) * 2 + c)

    def mod4(v):
        return lax.rem(v + 4, 4)

    x_right, x_left = at(x=mod4(mx + 1)), at(x=mod4(mx - 1))
    y_right, y_left = at(y=mod4(my + 1)), at(y=mod4(my - 1))
    z_right, z_left = at(z=mod4(mz + 1)), at(z=mod4(mz - 1))
    y_far, z_far = at(y=mod4(my + 2)), at(z=mod4(mz + 2))
    sibling = at(c=1 - mc)
    partner = at(zl=1 - ml)

    count = [0]
    unsent = []
    unsent_weights = []

    def send(src, dst, device, pending=unsent):
        i = count[0]
        count[0] += 1
        copy = pltpu.make_async_remote_copy(
            src_ref=src, dst_ref=dst, send_sem=ssem.at[i], recv_sem=rsem.at[i],
            device_id=device, device_id_type=MESH,
        )
        copy.start()
        pending.append(copy)
        return copy

    def drain(pending=unsent):
        for copy in pending:
            copy.wait_send()
        pending.clear()

    def send_weights(src, dst, device):
        return send(src, dst, device, unsent_weights)

    own = act.at[mz, mc, my, pl.ds(0, T)]
    loads = [
        pltpu.make_async_copy(tok_in, own, lsem.at[0]),
        pltpu.make_async_copy(down1_in, down1.at[rep], lsem.at[1]),
        pltpu.make_async_copy(down2_in, down2.at[rep], lsem.at[2]),
    ]
    for load in loads:
        load.start()

    order = [mz, mod4(mz - 1), mod4(mz + 1), mod4(mz + 2)]
    n_piece = CAP // RAW
    n_raw = n_piece + D // RAW

    def raw_copy(i):
        if i < n_piece:
            src = piece_in.at[pl.ds(i * RAW, RAW)]
        else:
            j = i - n_piece
            src = gate_up.at[pl.ds(pl.multiple_of(order[j // 4] * 1024 + (j % 4) * RAW, RAW), RAW)]
        return pltpu.make_async_copy(src, raw.at[i % RAW_SLOTS], raw_sem.at[i % RAW_SLOTS])

    for i in range(RAW_SLOTS):
        raw_copy(i).start()

    row = lax.broadcasted_iota(jnp.int32, (16, 128), 0)
    terms = jnp.zeros((16, 128), F32)
    for i in range(2):
        rest = head[pl.ds(i, 1), :]
        for j in range(3):
            part = rest.astype(BF).astype(F32)
            terms = jnp.where(row == 3 * i + j, part, terms)
            rest = rest - part
    act[mz, mc, my, pl.ds(T, 16), :] = terms.astype(BF)

    barrier = pltpu.get_barrier_semaphore()
    neighbours = (
        x_right, x_left, y_right, y_left, y_far, z_right, z_left, z_far, sibling, partner,
    )
    for n in neighbours:
        pl.semaphore_signal(barrier, inc=1, device_id=n, device_id_type=MESH)

    done = [0]

    def relay(n):
        for _ in range(n):
            i = done[0]
            if i >= n_raw:
                return
            done[0] += 1
            raw_copy(i).wait()
            slot = i % RAW_SLOTS

            def step(k, _):
                rows = pl.ds(pl.multiple_of(k * 64, 64), 64)
                flat = raw[slot, rows].reshape(64, 2 * W)
                if i < n_piece:
                    pcs[rep, pl.ds(pl.multiple_of(i * RAW + k * 64, 64), 64), :] = flat
                else:
                    j = i - n_piece
                    base = order[j // 4] * 1024 + (j % 4) * RAW + k * 64
                    wprev[pl.ds(pl.multiple_of(base, 64), 64), :] = flat
                return 0

            lax.fori_loop(0, RAW // 64, step, 0)
            if i + RAW_SLOTS < n_raw:
                raw_copy(i + RAW_SLOTS).start()

    def gather(buf, first, rows):
        half = rows // 2

        def whole_of(b):
            return buf.at[b, pl.ds(first, rows)]

        def halves(b):
            return buf.at[b, pl.ds(first, half)], buf.at[b, pl.ds(first + half, half)]

        left, right, far = mod4(mx - 1), mod4(mx + 1), mod4(mx + 2)
        me = ml * 4
        other = (1 - ml) * 4
        h = {}

        def start_z():
            b = whole_of(me + mx)
            h["p"] = send_weights(b, b, partner)

        def start_x():
            b = whole_of(me + mx)
            h["r"] = send_weights(b, b, x_right)
            h["l"] = send_weights(b, b, x_left)

        def forward():
            h["r"].wait_recv()
            a, _ = halves(me + left)
            h["ra"] = send_weights(a, a, x_right)
            h["l"].wait_recv()
            _, b = halves(me + right)
            h["lb"] = send_weights(b, b, x_left)

        def relay_partner():
            h["p"].wait_recv()
            b = whole_of(other + mx)
            h["pr"] = send_weights(b, b, x_right)
            h["pl"] = send_weights(b, b, x_left)

        def far_to_partner():
            h["ra"].wait_recv()
            h["lb"].wait_recv()
            b = whole_of(me + far)
            h["pf"] = send_weights(b, b, partner)

        def far_by_x():
            h["pr"].wait_recv()
            a, _ = halves(other + left)
            h["pra"] = send_weights(a, a, x_right)
            h["pl"].wait_recv()
            _, b = halves(other + right)
            h["plb"] = send_weights(b, b, x_left)

        def wait(*names):
            for n in names:
                h[n].wait_recv()

        return {
            "start_x": start_x, "start_z": start_z, "forward": forward,
            "partner": relay_partner, "far": far_to_partner, "far_x": far_by_x, "wait": wait,
        }

    g1 = gather(down1, 0, W)
    ga, gb, gc = (gather(pcs, k * 256, 256) for k in range(3))
    g2 = gather(down2, 0, W)

    def blk(q, y=my):
        return act.at[q, mc, y]

    def half_a(ref):
        return ref.at[pl.ds(0, H)]

    def half_b(ref):
        return ref.at[pl.ds(H, H)]

    def rest_b(ref):
        return ref.at[pl.ds(H, ROWS - H)]

    def activations():
        h = {}
        qz = dict(zip(("own", "left", "right", "far"), order))

        def y_start(k):
            b = blk(qz[k])
            h[k, "r"] = send(b, b, y_right)
            h[k, "l"] = send(b, b, y_left)

        def y_forward(k):
            h[k, "r"].wait_recv()
            a = half_a(blk(qz[k], mod4(my - 1)))
            h[k, "ra"] = send(a, a, y_right)
            h[k, "l"].wait_recv()
            b = rest_b(blk(qz[k], mod4(my + 1)))
            h[k, "lb"] = send(b, b, y_left)

        def y_end(k):
            h[k, "ra"].wait_recv()
            h[k, "lb"].wait_recv()
            b = act.at[qz[k], mc]
            h[k, "c"] = send(b, b, sibling)

        def z_start():
            b = blk(mz)
            h["r"] = send(b, b, z_right)
            h["l"] = send(b, b, z_left)

        def z_left_in():
            h["r"].wait_recv()
            a = half_a(blk(qz["left"]))
            h["ra"] = send(a, a, z_right)

        def z_right_in():
            h["l"].wait_recv()
            b = rest_b(blk(qz["right"]))
            h["lb"] = send(b, b, z_left)

        def z_end():
            h["ra"].wait_recv()
            h["lb"].wait_recv()

        def whole(k):
            h[k, "c"].wait_recv()

        return y_start, y_forward, y_end, z_start, z_left_in, z_right_in, z_end, whole

    def scaled(q, gain):
        def step(i, _):
            v = act[q, lax.rem(i, 2), i // 2, pl.ds(0, T), :].astype(F32)
            g = gain[pl.ds(q * 8 + i, 1), :]
            nbuf[:, pl.ds(pl.multiple_of(i * 128, 128), 128)] = (v * g).astype(BF)
            sumsq[...] += v * v
            return 0

        lax.fori_loop(0, 8, step, 0)

    def mm_prev(q):
        rows = pl.ds(pl.multiple_of(q * 1024, 1024), 1024)

        def step(j, _):
            cols = pl.ds(pl.multiple_of(j * 256, 256), 256)
            both[:, cols] += jnp.dot(nbuf[...], wprev[rows, cols], preferred_element_type=F32)
            return 0

        lax.fori_loop(0, 4, step, 0)

    def permute(q, first):
        def step(i, _):
            r, k = i // 3 * 2 + mc, lax.rem(i, 3)
            lanes = pl.ds(pl.multiple_of((r * 3 + k) * 256, 256), 256)
            want = slots[:, lanes] - q * 1024
            moved = jnp.zeros((T, 256), F32)
            for j in range(4):
                near = (want - j * 256).astype(F32).astype(BF)
                pick = jnp.where(rowid[...] == near, 1.0, 0.0).astype(BF)
                moved += jnp.dot(nbuf[:, j * 256 : j * 256 + 256], pick, preferred_element_type=F32)
            if first:
                nperm[r, k] = moved.astype(BF)
            else:
                nperm[r, k] = (nperm[r, k].astype(F32) + moved).astype(BF)
            return 0

        lax.fori_loop(0, SLOTS // 512, step, 0)

    def mm_pieces(k):
        def step(j, _):
            cols = pl.ds(pl.multiple_of(j * 256, 256), 256)
            total = both[:, cols]
            for r in range(8):
                total += jnp.dot(
                    nperm[r, k], pcs[r, pl.ds(k * 256, 256), cols], preferred_element_type=F32
                )
            both[:, cols] = total
            return 0

        lax.fori_loop(0, 4, step, 0)

    def hidden():
        def step(i, _):
            rows = pl.ds(pl.multiple_of(i * 64, 64), 64)
            mean = jnp.sum(sumsq[rows, :], axis=1, keepdims=True) * (1.0 / D)
            scale = lax.rsqrt(mean + 1e-06)
            g = both[rows, pl.ds(0, W)] * scale
            u = both[rows, pl.ds(W, W)] * scale
            hid[rows, :] = (g / (1.0 + jnp.exp(-g)) * u).astype(BF)
            return 0

        lax.fori_loop(0, T // 64, step, 0)

    def reset():
        both[...] = jnp.zeros_like(both)
        sumsq[...] = jnp.zeros_like(sumsq)

    def add(dst, *srcs):
        total = dst[...].astype(F32)
        for s in srcs:
            total += s[...].astype(F32)
        dst[...] = total.astype(BF)

    def reduce(down, ready, extra):
        groups = [mod4(mz + 2), mod4(mz + 1), mod4(mz - 1), mz]
        c_in = {}
        t_in = {}
        y_in = {}
        z_in = {}

        def mult(k):
            q = groups[k]
            ready(k)

            def step(y, _):
                cols = pl.ds(pl.multiple_of(lax.rem(y, 2) * 256, 256), 256)
                term = jnp.dot(hid[...], down[q * 2 + y // 2, :, cols], preferred_element_type=F32)
                prt[q, 0, y] = term[:, :128].astype(BF)
                prt[q, 1, y] = term[:, 128:].astype(BF)
                return 0

            lax.fori_loop(0, 4, step, 0)
            c_in[k] = send(prt.at[q, 1 - mc], rs_c.at[k], sibling)

        def cores(k):
            q = groups[k]
            c_in[k].wait_recv()

            def step(y, _):
                add(prt.at[q, mc, y], rs_c.at[k, y])
                return 0

            lax.fori_loop(0, 4, step, 0)
            far = prt.at[q, mc, mod4(my + 2)]
            t_in[k] = (
                send(half_a(far), yt_l.at[k], y_right),
                send(half_b(far), yt_r.at[k], y_left),
            )

        def y_pass(k):
            q = groups[k]
            t_in[k][0].wait_recv()
            right = prt.at[q, mc, mod4(my + 1)]
            add(half_a(right), yt_l.at[k])
            first = send(right, y_l.at[k], y_right)
            t_in[k][1].wait_recv()
            left = prt.at[q, mc, mod4(my - 1)]
            add(half_b(left), yt_r.at[k])
            second = send(left, y_r.at[k], y_left)
            y_in[k] = (first, second)

        def y_last(k):
            q = groups[k]
            y_in[k][0].wait_recv()
            y_in[k][1].wait_recv()
            mine = prt.at[q, mc, my]
            add(mine, y_l.at[k], y_r.at[k])
            if k == 0:
                z_in["a"] = send(half_a(mine), zt_l, z_right)
                z_in["b"] = send(half_b(mine), zt_r, z_left)
            elif k == 1:
                z_in["a"].wait_recv()
                add(half_a(mine), zt_l)
                z_in["l"] = send(mine, z_l, z_right)
            elif k == 2:
                z_in["b"].wait_recv()
                add(half_b(mine), zt_r)
                z_in["r"] = send(mine, z_r, z_left)
            else:
                z_in["l"].wait_recv()
                z_in["r"].wait_recv()

        mult(0)
        mult(1)
        cores(0)
        mult(2)
        cores(1)
        y_pass(0)
        mult(3)
        cores(2)
        y_pass(1)
        y_last(0)
        cores(3)
        extra(0)
        y_pass(2)
        y_last(1)
        y_pass(3)
        extra(1)
        y_last(2)
        extra(2)
        y_last(3)
        total = own[...].astype(F32) + prt[mz, mc, my].astype(F32)
        return (total + z_l[...].astype(F32) + z_r[...].astype(F32)).astype(BF)

    reset()
    rowid[...] = lax.broadcasted_iota(jnp.int32, (256, 256), 0).astype(F32).astype(BF)
    pl.semaphore_wait(barrier, len(neighbours))
    loads[0].wait()
    y_start, y_forward, y_end, z_start, z_left_in, z_right_in, z_end, whole = activations()
    z_start()
    y_start("own")
    loads[1].wait()
    g1["start_x"]()
    relay(3)
    ga["start_x"]()
    z_left_in()
    y_start("left")
    z_right_in()
    y_start("right")
    relay(1)
    y_forward("own")
    z_end()
    g1["start_z"]()
    y_start("far")
    relay(1)
    y_forward("left")
    g1["forward"]()
    relay(1)
    y_end("own")
    y_forward("right")
    relay(1)
    y_end("left")
    relay(1)
    y_forward("far")
    relay(1)
    y_end("right")
    g1["partner"]()
    gb["start_x"]()
    relay(1)
    y_end("far")
    g1["far"]()
    ga["start_z"]()
    relay(9)
    loads[2].wait()
    whole("own")
    scaled(order[0], gain1)
    mm_prev(order[0])
    whole("left")
    scaled(order[1], gain1)
    mm_prev(order[1])
    gc["start_x"]()
    gb["start_z"]()
    whole("right")
    scaled(order[2], gain1)
    mm_prev(order[2])
    whole("far")
    scaled(order[3], gain1)
    mm_prev(order[3])
    hidden()
    drain()

    def ready1(k):
        if k == 0:
            g1["wait"]("pr", "pl", "pf")

    def extra1(k):
        if k == 0:
            ga["forward"]()
            ga["partner"]()
        if k == 1:
            g2["start_x"]()

    middle = reduce(down1, ready1, extra1)
    own[...] = middle

    reset()
    y_start, y_forward, y_end, z_start, z_left_in, z_right_in, z_end, whole = activations()
    z_start()
    y_start("own")
    z_left_in()
    y_start("left")
    z_right_in()
    y_start("right")
    y_forward("own")
    y_forward("left")
    z_end()
    y_start("far")
    gc["start_z"]()
    gb["forward"]()
    gb["partner"]()
    y_end("own")
    y_forward("right")
    ga["far"]()
    y_end("left")
    whole("own")
    scaled(order[0], gain2)
    permute(order[0], True)
    y_forward("far")
    y_end("right")
    g2["start_z"]()
    gc["forward"]()
    whole("left")
    scaled(order[1], gain2)
    permute(order[1], False)
    y_end("far")
    gc["partner"]()
    gb["far"]()
    whole("right")
    scaled(order[2], gain2)
    permute(order[2], False)
    g2["forward"]()
    gc["far"]()
    whole("far")
    scaled(order[3], gain2)
    permute(order[3], False)
    moved = []
    for i in range(4):
        part = nperm.at[i * 2 + mc]
        moved.append(send(part, part, sibling))
    g2["partner"]()
    for m in moved:
        m.wait_recv()
    for k, g in enumerate((ga, gb, gc)):
        g["wait"]("pr", "pl", "pf")
        mm_pieces(k)
    g2["far_x"]()
    hidden()
    drain()

    def ready2(k):
        if k == 0:
            g2["wait"]("ra", "lb", "pra", "plb")

    logit_in = []

    def total_of(base):
        lgs[base + 4] = (lgs[base] + lgs[base + 3]) + (lgs[base + 1] + lgs[base + 2])

    def exchange(base, right, left, far):
        for i, device in enumerate((right, left, far)):
            logit_in.append(send(lgs.at[base], lgs.at[base + 1 + i], device))

    def arrive():
        for copy in logit_in:
            copy.wait_recv()
        logit_in.clear()

    def extra2(k):
        if k == 0:
            score[...] = jnp.zeros_like(score)

            def step(r, _):
                parts = [
                    act[r // 2, j % 2, lax.rem(r, 2) * 2 + j // 2, pl.ds(T, 16), :] for j in range(4)
                ]
                score[...] += lax.dot_general(
                    down2[r], jnp.concatenate(parts, axis=1), (((1,), (1,)), ((), ())),
                    preferred_element_type=F32,
                )
                return 0

            lax.fori_loop(0, 8, step, 0)
            rows = lax.broadcasted_iota(jnp.int32, (T, 24), 0)
            pick = jnp.where(rows == pos[...], 1.0, 0.0).astype(BF)
            tall = (((0,), (0,)), ((), ()))
            mids = lax.dot_general(pick, own[...], tall, preferred_element_type=F32)
            hids = lax.dot_general(pick, hid[...], tall, preferred_element_type=F32)
            six = jnp.dot(
                hids, score[...], precision=lax.Precision.HIGHEST, preferred_element_type=F32
            )
            lane = lax.broadcasted_iota(jnp.int32, (24, 128), 1)
            both_logits = jnp.zeros((24, 128), F32)
            for i in range(2):
                value = jnp.sum(mids * head[pl.ds(i, 1), :], axis=1, keepdims=True)
                for j in range(3):
                    value += six[:, 3 * i + j : 3 * i + j + 1]
                both_logits = jnp.where(lane == i, value, both_logits)
            lgs[0] = both_logits
            logit_in.append(send(lgs.at[0], lgs.at[1], sibling))
        if k == 1:
            arrive()
            lgs[2] = lgs[0] + lgs[1]
            exchange(2, y_right, y_left, y_far)
        if k == 2:
            arrive()
            total_of(2)
            exchange(6, z_right, z_left, z_far)

    out[...] = reduce(down2, ready2, extra2)
    arrive()
    total_of(6)
    logits[...] = lgs[10][:, :2]
    drain()
    drain(unsent_weights)


def shards(
    tokens, prev_gain, prev_gate_up, prev_down, next_gain, piece_buffer, slot_rows, next_down,
    score_head, step_positions,
):
    hbm = pl.BlockSpec(memory_space=pl.ANY)
    vmem = pl.BlockSpec(memory_space=pltpu.VMEM)
    dma = pltpu.SemaphoreType.DMA
    block = (T, 128)
    return pl.pallas_call(
        kernel,
        out_shape=(
            jax.ShapeDtypeStruct((T, 128), BF),
            jax.ShapeDtypeStruct((24, 2), F32),
        ),
        in_specs=[hbm, vmem, hbm, hbm, vmem, hbm, vmem, hbm, vmem, vmem],
        out_specs=(vmem, vmem),
        scratch_shapes=[
            pltpu.VMEM((4, 2, 4, ROWS, 128), BF),
            pltpu.VMEM((W, 16), F32),
            pltpu.VMEM((D, 2 * W), BF),
            pltpu.VMEM((RAW_SLOTS, RAW, 2, W), BF),
            pltpu.VMEM((8, W, 512), BF),
            pltpu.VMEM((8, W, 512), BF),
            pltpu.VMEM((8, CAP, 2 * W), BF),
            pltpu.VMEM((8, 3, T, 256), BF),
            pltpu.VMEM((256, 256), BF),
            pltpu.VMEM((T, 1024), BF),
            pltpu.VMEM((T, 2 * W), F32),
            pltpu.VMEM((T, W), BF),
            pltpu.VMEM(block, F32),
            pltpu.VMEM((4, 2, 4) + block, BF),
            pltpu.VMEM((4, 4) + block, BF),
            pltpu.VMEM((4,) + block, BF),
            pltpu.VMEM((4,) + block, BF),
            pltpu.VMEM((4, H, 128), BF),
            pltpu.VMEM((4, H, 128), BF),
            pltpu.VMEM(block, BF),
            pltpu.VMEM(block, BF),
            pltpu.VMEM((H, 128), BF),
            pltpu.VMEM((H, 128), BF),
            pltpu.VMEM((11, 24, 128), F32),
            dma((N_SEM,)),
            dma((N_SEM,)),
            dma((3,)),
            dma((RAW_SLOTS,)),
        ],
        compiler_params=pltpu.CompilerParams(
            collective_id=0, has_side_effects=True, vmem_limit_bytes=62 * 2**20
        ),
        cost_estimate=pl.CostEstimate(
            flops=2 * T * (D * 1024 + SLOTS * 1024 + D * SLOTS + 2 * 512 * D),
            bytes_accessed=16 * 2**20, transcendentals=2 * T * W,
        ),
    )(
        tokens,
        prev_gain.reshape(32, 128),
        prev_gate_up,
        prev_down,
        next_gain.reshape(32, 128),
        piece_buffer,
        slot_rows.reshape(1, SLOTS),
        next_down,
        score_head.T,
        step_positions.reshape(1, 24),
    )


def solution(mesh):
    in_specs = (
        P("replica", "tensor"),
        P(),
        P(None, None, "tensor"),
        P("tensor", "replica"),
        P(),
        P("replica", None, "tensor"),
        P(),
        P("tensor", "replica"),
        P("tensor", None),
        P("replica"),
    )
    out_specs = (P("replica", "tensor"), P("replica", None))
    return jax.shard_map(shards, mesh=mesh, in_specs=in_specs, out_specs=out_specs, check_vma=False)
```

```python
import jax
import jax.numpy as jnp
from jax import lax
from jax.experimental import pallas as pl
from jax.experimental.pallas import tpu as pltpu
from jax.sharding import PartitionSpec as P

MESH = pl.DeviceIdType.MESH
BF = jnp.bfloat16
F32 = jnp.float32
D = 4096
T = 512
H = T // 2
ROWS = T + 16
W = 512
CAP = 768
SLOTS = 8 * CAP
N_SEM = 192
RAW = 256
RAW_SLOTS = 4


def kernel(
    tok_in, gain1, gate_up, down1_in, gain2, piece_in, slots, down2_in, head, pos,
    out, logits,
    act, score, wprev, raw, down1, down2, pcs, nperm, rowid, nbuf, both, hid, sumsq,
    prt, rs_c, y_l, y_r, yt_l, yt_r, z_l, z_r, zt_l, zt_r, lgs,
    ssem, rsem, lsem, raw_sem,
):
    rep = lax.axis_index("replica")
    ten = lax.axis_index("tensor")
    ml, mx = rep // 4, rep % 4
    mz, my, mc = ten // 8, (ten // 2) % 4, ten % 2

    def at(zl=ml, x=mx, z=mz, y=my, c=mc):
        return (zl * 4 + x, (z * 4 + y) * 2 + c)

    def mod4(v):
        return lax.rem(v + 4, 4)

    x_right, x_left = at(x=mod4(mx + 1)), at(x=mod4(mx - 1))
    y_right, y_left = at(y=mod4(my + 1)), at(y=mod4(my - 1))
    z_right, z_left = at(z=mod4(mz + 1)), at(z=mod4(mz - 1))
    y_far, z_far = at(y=mod4(my + 2)), at(z=mod4(mz + 2))
    sibling = at(c=1 - mc)
    partner = at(zl=1 - ml)

    count = [0]
    unsent = []
    unsent_weights = []

    def send(src, dst, device, pending=unsent):
        i = count[0]
        count[0] += 1
        copy = pltpu.make_async_remote_copy(
            src_ref=src, dst_ref=dst, send_sem=ssem.at[i], recv_sem=rsem.at[i],
            device_id=device, device_id_type=MESH,
        )
        copy.start()
        pending.append(copy)
        return copy

    def drain(pending=unsent):
        for copy in pending:
            copy.wait_send()
        pending.clear()

    def send_weights(src, dst, device):
        return send(src, dst, device, unsent_weights)

    own = act.at[mz, mc, my, pl.ds(0, T)]
    loads = [
        pltpu.make_async_copy(tok_in, own, lsem.at[0]),
        pltpu.make_async_copy(down1_in, down1.at[rep], lsem.at[1]),
        pltpu.make_async_copy(down2_in, down2.at[rep], lsem.at[2]),
    ]
    for load in loads:
        load.start()

    order = [mz, mod4(mz - 1), mod4(mz + 1), mod4(mz + 2)]
    n_piece = CAP // RAW
    n_raw = n_piece + D // RAW

    def raw_copy(i):
        if i < n_piece:
            src = piece_in.at[pl.ds(i * RAW, RAW)]
        else:
            j = i - n_piece
            src = gate_up.at[pl.ds(pl.multiple_of(order[j // 4] * 1024 + (j % 4) * RAW, RAW), RAW)]
        return pltpu.make_async_copy(src, raw.at[i % RAW_SLOTS], raw_sem.at[i % RAW_SLOTS])

    for i in range(RAW_SLOTS):
        raw_copy(i).start()

    row = lax.broadcasted_iota(jnp.int32, (16, 128), 0)
    terms = jnp.zeros((16, 128), F32)
    for i in range(2):
        rest = head[pl.ds(i, 1), :]
        for j in range(3):
            part = rest.astype(BF).astype(F32)
            terms = jnp.where(row == 3 * i + j, part, terms)
            rest = rest - part
    act[mz, mc, my, pl.ds(T, 16), :] = terms.astype(BF)

    barrier = pltpu.get_barrier_semaphore()
    neighbours = (
        x_right, x_left, y_right, y_left, y_far, z_right, z_left, z_far, sibling, partner,
    )
    for n in neighbours:
        pl.semaphore_signal(barrier, inc=1, device_id=n, device_id_type=MESH)

    done = [0]

    def relay(n):
        for _ in range(n):
            i = done[0]
            if i >= n_raw:
                return
            done[0] += 1
            raw_copy(i).wait()
            slot = i % RAW_SLOTS

            def step(k, _):
                rows = pl.ds(pl.multiple_of(k * 64, 64), 64)
                flat = raw[slot, rows].reshape(64, 2 * W)
                if i < n_piece:
                    pcs[rep, pl.ds(pl.multiple_of(i * RAW + k * 64, 64), 64), :] = flat
                else:
                    j = i - n_piece
                    base = order[j // 4] * 1024 + (j % 4) * RAW + k * 64
                    wprev[pl.ds(pl.multiple_of(base, 64), 64), :] = flat
                return 0

            lax.fori_loop(0, RAW // 64, step, 0)
            if i + RAW_SLOTS < n_raw:
                raw_copy(i + RAW_SLOTS).start()

    def gather(buf, first, rows):
        half = rows // 2

        def whole_of(b):
            return buf.at[b, pl.ds(first, rows)]

        def halves(b):
            return buf.at[b, pl.ds(first, half)], buf.at[b, pl.ds(first + half, half)]

        left, right, far = mod4(mx - 1), mod4(mx + 1), mod4(mx + 2)
        me = ml * 4
        other = (1 - ml) * 4
        h = {}

        def start_z():
            b = whole_of(me + mx)
            h["p"] = send_weights(b, b, partner)

        def start_x():
            b = whole_of(me + mx)
            h["r"] = send_weights(b, b, x_right)
            h["l"] = send_weights(b, b, x_left)

        def forward():
            h["r"].wait_recv()
            a, _ = halves(me + left)
            h["ra"] = send_weights(a, a, x_right)
            h["l"].wait_recv()
            _, b = halves(me + right)
            h["lb"] = send_weights(b, b, x_left)

        def relay_partner():
            h["p"].wait_recv()
            b = whole_of(other + mx)
            h["pr"] = send_weights(b, b, x_right)
            h["pl"] = send_weights(b, b, x_left)

        def far_to_partner():
            h["ra"].wait_recv()
            h["lb"].wait_recv()
            b = whole_of(me + far)
            h["pf"] = send_weights(b, b, partner)

        def far_by_x():
            h["pr"].wait_recv()
            a, _ = halves(other + left)
            h["pra"] = send_weights(a, a, x_right)
            h["pl"].wait_recv()
            _, b = halves(other + right)
            h["plb"] = send_weights(b, b, x_left)

        def wait(*names):
            for n in names:
                h[n].wait_recv()

        return {
            "start_x": start_x, "start_z": start_z, "forward": forward,
            "partner": relay_partner, "far": far_to_partner, "far_x": far_by_x, "wait": wait,
        }

    g1 = gather(down1, 0, W)
    ga, gb, gc = (gather(pcs, k * 256, 256) for k in range(3))
    g2 = gather(down2, 0, W)

    def blk(q, y=my):
        return act.at[q, mc, y]

    def half_a(ref):
        return ref.at[pl.ds(0, H)]

    def half_b(ref):
        return ref.at[pl.ds(H, H)]

    def rest_b(ref):
        return ref.at[pl.ds(H, ROWS - H)]

    def activations():
        h = {}
        qz = dict(zip(("own", "left", "right", "far"), order))

        def y_start(k):
            b = blk(qz[k])
            h[k, "r"] = send(b, b, y_right)
            h[k, "l"] = send(b, b, y_left)

        def y_forward(k):
            h[k, "r"].wait_recv()
            a = half_a(blk(qz[k], mod4(my - 1)))
            h[k, "ra"] = send(a, a, y_right)
            h[k, "l"].wait_recv()
            b = rest_b(blk(qz[k], mod4(my + 1)))
            h[k, "lb"] = send(b, b, y_left)

        def y_end(k):
            h[k, "ra"].wait_recv()
            h[k, "lb"].wait_recv()
            b = act.at[qz[k], mc]
            h[k, "c"] = send(b, b, sibling)

        def z_start():
            b = blk(mz)
            h["r"] = send(b, b, z_right)
            h["l"] = send(b, b, z_left)

        def z_left_in():
            h["r"].wait_recv()
            a = half_a(blk(qz["left"]))
            h["ra"] = send(a, a, z_right)

        def z_right_in():
            h["l"].wait_recv()
            b = rest_b(blk(qz["right"]))
            h["lb"] = send(b, b, z_left)

        def z_end():
            h["ra"].wait_recv()
            h["lb"].wait_recv()

        def whole(k):
            h[k, "c"].wait_recv()

        return y_start, y_forward, y_end, z_start, z_left_in, z_right_in, z_end, whole

    def scaled(q, gain):
        def step(i, _):
            v = act[q, lax.rem(i, 2), i // 2, pl.ds(0, T), :].astype(F32)
            g = gain[pl.ds(q * 8 + i, 1), :]
            nbuf[:, pl.ds(pl.multiple_of(i * 128, 128), 128)] = (v * g).astype(BF)
            sumsq[...] += v * v
            return 0

        lax.fori_loop(0, 8, step, 0)

    def mm_prev(q):
        rows = pl.ds(pl.multiple_of(q * 1024, 1024), 1024)

        def step(j, _):
            cols = pl.ds(pl.multiple_of(j * 256, 256), 256)
            both[:, cols] += jnp.dot(nbuf[...], wprev[rows, cols], preferred_element_type=F32)
            return 0

        lax.fori_loop(0, 4, step, 0)

    def permute(q, first):
        def step(i, _):
            r, k = i // 3 * 2 + mc, lax.rem(i, 3)
            lanes = pl.ds(pl.multiple_of((r * 3 + k) * 256, 256), 256)
            want = slots[:, lanes] - q * 1024
            moved = jnp.zeros((T, 256), F32)
            for j in range(4):
                near = (want - j * 256).astype(F32).astype(BF)
                pick = jnp.where(rowid[...] == near, 1.0, 0.0).astype(BF)
                moved += jnp.dot(nbuf[:, j * 256 : j * 256 + 256], pick, preferred_element_type=F32)
            if first:
                nperm[r, k] = moved.astype(BF)
            else:
                nperm[r, k] = (nperm[r, k].astype(F32) + moved).astype(BF)
            return 0

        lax.fori_loop(0, SLOTS // 512, step, 0)

    def mm_pieces(k):
        def step(j, _):
            cols = pl.ds(pl.multiple_of(j * 256, 256), 256)
            total = both[:, cols]
            for r in range(8):
                total += jnp.dot(
                    nperm[r, k], pcs[r, pl.ds(k * 256, 256), cols], preferred_element_type=F32
                )
            both[:, cols] = total
            return 0

        lax.fori_loop(0, 4, step, 0)

    def hidden():
        def step(i, _):
            rows = pl.ds(pl.multiple_of(i * 64, 64), 64)
            mean = jnp.sum(sumsq[rows, :], axis=1, keepdims=True) * (1.0 / D)
            scale = lax.rsqrt(mean + 1e-06)
            g = both[rows, pl.ds(0, W)] * scale
            u = both[rows, pl.ds(W, W)] * scale
            hid[rows, :] = (g / (1.0 + jnp.exp(-g)) * u).astype(BF)
            return 0

        lax.fori_loop(0, T // 64, step, 0)

    def reset():
        both[...] = jnp.zeros_like(both)
        sumsq[...] = jnp.zeros_like(sumsq)

    def add(dst, *srcs):
        total = dst[...].astype(F32)
        for s in srcs:
            total += s[...].astype(F32)
        dst[...] = total.astype(BF)

    def reduce(down, ready, extra):
        groups = [mod4(mz + 2), mod4(mz + 1), mod4(mz - 1), mz]
        c_in = {}
        t_in = {}
        y_in = {}
        z_in = {}

        def mult(k):
            q = groups[k]
            ready(k)

            def step(y, _):
                cols = pl.ds(pl.multiple_of(lax.rem(y, 2) * 256, 256), 256)
                term = jnp.dot(hid[...], down[q * 2 + y // 2, :, cols], preferred_element_type=F32)
                prt[q, 0, y] = term[:, :128].astype(BF)
                prt[q, 1, y] = term[:, 128:].astype(BF)
                return 0

            lax.fori_loop(0, 4, step, 0)
            c_in[k] = send(prt.at[q, 1 - mc], rs_c.at[k], sibling)

        def cores(k):
            q = groups[k]
            c_in[k].wait_recv()

            def step(y, _):
                add(prt.at[q, mc, y], rs_c.at[k, y])
                return 0

            lax.fori_loop(0, 4, step, 0)
            far = prt.at[q, mc, mod4(my + 2)]
            t_in[k] = (
                send(half_a(far), yt_l.at[k], y_right),
                send(half_b(far), yt_r.at[k], y_left),
            )

        def y_pass(k):
            q = groups[k]
            t_in[k][0].wait_recv()
            right = prt.at[q, mc, mod4(my + 1)]
            add(half_a(right), yt_l.at[k])
            first = send(right, y_l.at[k], y_right)
            t_in[k][1].wait_recv()
            left = prt.at[q, mc, mod4(my - 1)]
            add(half_b(left), yt_r.at[k])
            second = send(left, y_r.at[k], y_left)
            y_in[k] = (first, second)

        def y_last(k):
            q = groups[k]
            y_in[k][0].wait_recv()
            y_in[k][1].wait_recv()
            mine = prt.at[q, mc, my]
            add(mine, y_l.at[k], y_r.at[k])
            if k == 0:
                z_in["a"] = send(half_a(mine), zt_l, z_right)
                z_in["b"] = send(half_b(mine), zt_r, z_left)
            elif k == 1:
                z_in["a"].wait_recv()
                add(half_a(mine), zt_l)
                z_in["l"] = send(mine, z_l, z_right)
            elif k == 2:
                z_in["b"].wait_recv()
                add(half_b(mine), zt_r)
                z_in["r"] = send(mine, z_r, z_left)
            else:
                z_in["l"].wait_recv()
                z_in["r"].wait_recv()

        mult(0)
        mult(1)
        cores(0)
        mult(2)
        cores(1)
        y_pass(0)
        mult(3)
        cores(2)
        y_pass(1)
        y_last(0)
        cores(3)
        extra(0)
        y_pass(2)
        y_last(1)
        y_pass(3)
        extra(1)
        y_last(2)
        extra(2)
        y_last(3)
        total = own[...].astype(F32) + prt[mz, mc, my].astype(F32)
        return (total + z_l[...].astype(F32) + z_r[...].astype(F32)).astype(BF)

    reset()
    rowid[...] = lax.broadcasted_iota(jnp.int32, (256, 256), 0).astype(F32).astype(BF)
    pl.semaphore_wait(barrier, len(neighbours))
    loads[0].wait()
    y_start, y_forward, y_end, z_start, z_left_in, z_right_in, z_end, whole = activations()
    z_start()
    y_start("own")
    loads[1].wait()
    g1["start_x"]()
    relay(3)
    ga["start_x"]()
    z_left_in()
    y_start("left")
    z_right_in()
    y_start("right")
    relay(1)
    y_forward("own")
    z_end()
    g1["start_z"]()
    y_start("far")
    relay(1)
    y_forward("left")
    g1["forward"]()
    relay(1)
    y_end("own")
    y_forward("right")
    relay(1)
    y_end("left")
    relay(1)
    y_forward("far")
    relay(1)
    y_end("right")
    g1["partner"]()
    gb["start_x"]()
    relay(1)
    y_end("far")
    g1["far"]()
    ga["start_z"]()
    relay(9)
    loads[2].wait()
    whole("own")
    scaled(order[0], gain1)
    mm_prev(order[0])
    whole("left")
    scaled(order[1], gain1)
    mm_prev(order[1])
    gc["start_x"]()
    gb["start_z"]()
    whole("right")
    scaled(order[2], gain1)
    mm_prev(order[2])
    whole("far")
    scaled(order[3], gain1)
    mm_prev(order[3])
    hidden()
    drain()

    def ready1(k):
        if k == 0:
            g1["wait"]("pr", "pl", "pf")

    def extra1(k):
        if k == 0:
            ga["forward"]()
            ga["partner"]()
        if k == 1:
            g2["start_x"]()

    middle = reduce(down1, ready1, extra1)
    own[...] = middle

    reset()
    y_start, y_forward, y_end, z_start, z_left_in, z_right_in, z_end, whole = activations()
    z_start()
    y_start("own")
    z_left_in()
    y_start("left")
    z_right_in()
    gc["start_z"]()
    y_start("right")
    y_forward("own")
    y_forward("left")
    z_end()
    y_start("far")
    gb["forward"]()
    gb["partner"]()
    y_end("own")
    y_forward("right")
    ga["far"]()
    y_end("left")
    whole("own")
    scaled(order[0], gain2)
    permute(order[0], True)
    y_forward("far")
    y_end("right")
    g2["start_z"]()
    gc["forward"]()
    whole("left")
    scaled(order[1], gain2)
    permute(order[1], False)
    y_end("far")
    gc["partner"]()
    gb["far"]()
    whole("right")
    scaled(order[2], gain2)
    permute(order[2], False)
    g2["forward"]()
    gc["far"]()
    whole("far")
    scaled(order[3], gain2)
    permute(order[3], False)
    moved = []
    for i in range(4):
        part = nperm.at[i * 2 + mc]
        moved.append(send(part, part, sibling))
    g2["partner"]()
    for m in moved:
        m.wait_recv()
    for k, g in enumerate((ga, gb, gc)):
        g["wait"]("pr", "pl", "pf")
        mm_pieces(k)
    g2["far_x"]()
    hidden()
    drain()

    def ready2(k):
        if k == 0:
            g2["wait"]("ra", "lb", "pra", "plb")

    logit_in = []

    def total_of(base):
        lgs[base + 4] = (lgs[base] + lgs[base + 3]) + (lgs[base + 1] + lgs[base + 2])

    def exchange(base, right, left, far):
        for i, device in enumerate((right, left, far)):
            logit_in.append(send(lgs.at[base], lgs.at[base + 1 + i], device))

    def arrive():
        for copy in logit_in:
            copy.wait_recv()
        logit_in.clear()

    def extra2(k):
        if k == 0:
            score[...] = jnp.zeros_like(score)

            def step(r, _):
                parts = [
                    act[r // 2, j % 2, lax.rem(r, 2) * 2 + j // 2, pl.ds(T, 16), :] for j in range(4)
                ]
                score[...] += lax.dot_general(
                    down2[r], jnp.concatenate(parts, axis=1), (((1,), (1,)), ((), ())),
                    preferred_element_type=F32,
                )
                return 0

            lax.fori_loop(0, 8, step, 0)
            rows = lax.broadcasted_iota(jnp.int32, (T, 24), 0)
            pick = jnp.where(rows == pos[...], 1.0, 0.0).astype(BF)
            tall = (((0,), (0,)), ((), ()))
            mids = lax.dot_general(pick, own[...], tall, preferred_element_type=F32)
            hids = lax.dot_general(pick, hid[...], tall, preferred_element_type=F32)
            six = jnp.dot(
                hids, score[...], precision=lax.Precision.HIGHEST, preferred_element_type=F32
            )
            lane = lax.broadcasted_iota(jnp.int32, (24, 128), 1)
            both_logits = jnp.zeros((24, 128), F32)
            for i in range(2):
                value = jnp.sum(mids * head[pl.ds(i, 1), :], axis=1, keepdims=True)
                for j in range(3):
                    value += six[:, 3 * i + j : 3 * i + j + 1]
                both_logits = jnp.where(lane == i, value, both_logits)
            lgs[0] = both_logits
            logit_in.append(send(lgs.at[0], lgs.at[1], sibling))
        if k == 1:
            arrive()
            lgs[2] = lgs[0] + lgs[1]
            exchange(2, y_right, y_left, y_far)
        if k == 2:
            arrive()
            total_of(2)
            exchange(6, z_right, z_left, z_far)

    out[...] = reduce(down2, ready2, extra2)
    arrive()
    total_of(6)
    logits[...] = lgs[10][:, :2]
    drain()
    drain(unsent_weights)


def shards(
    tokens, prev_gain, prev_gate_up, prev_down, next_gain, piece_buffer, slot_rows, next_down,
    score_head, step_positions,
):
    hbm = pl.BlockSpec(memory_space=pl.ANY)
    vmem = pl.BlockSpec(memory_space=pltpu.VMEM)
    dma = pltpu.SemaphoreType.DMA
    block = (T, 128)
    return pl.pallas_call(
        kernel,
        out_shape=(
            jax.ShapeDtypeStruct((T, 128), BF),
            jax.ShapeDtypeStruct((24, 2), F32),
        ),
        in_specs=[hbm, vmem, hbm, hbm, vmem, hbm, vmem, hbm, vmem, vmem],
        out_specs=(vmem, vmem),
        scratch_shapes=[
            pltpu.VMEM((4, 2, 4, ROWS, 128), BF),
            pltpu.VMEM((W, 16), F32),
            pltpu.VMEM((D, 2 * W), BF),
            pltpu.VMEM((RAW_SLOTS, RAW, 2, W), BF),
            pltpu.VMEM((8, W, 512), BF),
            pltpu.VMEM((8, W, 512), BF),
            pltpu.VMEM((8, CAP, 2 * W), BF),
            pltpu.VMEM((8, 3, T, 256), BF),
            pltpu.VMEM((256, 256), BF),
            pltpu.VMEM((T, 1024), BF),
            pltpu.VMEM((T, 2 * W), F32),
            pltpu.VMEM((T, W), BF),
            pltpu.VMEM(block, F32),
            pltpu.VMEM((4, 2, 4) + block, BF),
            pltpu.VMEM((4, 4) + block, BF),
            pltpu.VMEM((4,) + block, BF),
            pltpu.VMEM((4,) + block, BF),
            pltpu.VMEM((4, H, 128), BF),
            pltpu.VMEM((4, H, 128), BF),
            pltpu.VMEM(block, BF),
            pltpu.VMEM(block, BF),
            pltpu.VMEM((H, 128), BF),
            pltpu.VMEM((H, 128), BF),
            pltpu.VMEM((11, 24, 128), F32),
            dma((N_SEM,)),
            dma((N_SEM,)),
            dma((3,)),
            dma((RAW_SLOTS,)),
        ],
        compiler_params=pltpu.CompilerParams(
            collective_id=0, has_side_effects=True, vmem_limit_bytes=62 * 2**20
        ),
        cost_estimate=pl.CostEstimate(
            flops=2 * T * (D * 1024 + SLOTS * 1024 + D * SLOTS + 2 * 512 * D),
            bytes_accessed=16 * 2**20, transcendentals=2 * T * W,
        ),
    )(
        tokens,
        prev_gain.reshape(32, 128),
        prev_gate_up,
        prev_down,
        next_gain.reshape(32, 128),
        piece_buffer,
        slot_rows.reshape(1, SLOTS),
        next_down,
        score_head.T,
        step_positions.reshape(1, 24),
    )


def solution(mesh):
    in_specs = (
        P("replica", "tensor"),
        P(),
        P(None, None, "tensor"),
        P("tensor", "replica"),
        P(),
        P("replica", None, "tensor"),
        P(),
        P("tensor", "replica"),
        P("tensor", None),
        P("replica"),
    )
    out_specs = (P("replica", "tensor"), P("replica", None))
    return jax.shard_map(shards, mesh=mesh, in_specs=in_specs, out_specs=out_specs, check_vma=False)
```
